32 devices in a mesh: layer: 4 (over x, core), dp: 8 (over z, y).
Axes of the slice: x: 2, y: 2, z: 4, core: 2. Of those that a mesh axis runs over, the one named last changes fastest.
Arguments:
- acts: bfloat16 [4, 2048, 4096], P('layer', 'dp'), may hold values from -6 to 6
- factor_old: bfloat16 [4, 4096, 4096], P('layer', 'dp'), as said below
- basis_old: bfloat16 [4, 4096, 256], P('layer', 'dp'), may hold values from -0.09375 to 0.09375
- grads: bfloat16 [4, 4096, 2048], P(None, 'dp', 'layer'), may hold values from -12 to 12
Outputs:
- new_basis: bfloat16 [4, 4096, 256], P('layer', 'dp')
- eigenvalues: bfloat16 [4, 256], P('layer')
- preconditioned: bfloat16 [4, 4096, 2048], P(None, 'dp', 'layer')
- applied_rows: float32 [4, 4096, 256], P('layer', 'dp')
The draws below stay inside these ranges and needn't reach their ends.
Inputs may be any that keep to these rules, and one draw needn't show every extreme that they name: `factor_old`: each block is symmetric with a positive diagonal that outweighs the spectral norm of its off-diagonal part.
All inputs are finite; a program needn't handle non-finite values.
Results may differ from the reference program's by a relative error of at most 0.0035.
Values may be sent and summed in bfloat16 or wider, within the bound.
A program may use at most 64 MiB of HBM per device.

```python
import math
import jax
import jax.numpy as jnp
from jax import lax

BW = 4096
RANK = 256
OUTW = 2048
BLOCKS = 4
TOKENS = 2048


def draw_factor_old(key, part):
    key = jax.random.fold_in(key, 11)
    first_key, second_key = jax.random.split(key)
    raw = jax.random.normal(first_key, (BLOCKS, BW, BW), jnp.float32)
    upper = math.log(10.0)
    symmetric = (raw + jnp.swapaxes(raw, 1, 2)) * (0.2 / math.sqrt(2.0 * BW))
    diagonal = jnp.exp(jax.random.uniform(second_key, (BLOCKS, BW), jnp.float32, 0.0, upper))
    identity = jnp.eye(BW, dtype=jnp.float32)
    return (symmetric * (1.0 - identity) + diagonal[:, :, None] * identity).astype(jnp.bfloat16)


def raised(drawn, own_key, source, target, shards_of, factor):
    owner, partner = [(jnp.arange(drawn.shape[position]) // (drawn.shape[position] // shards_of)).reshape([-1 if axis == position else 1 for axis in range(drawn.ndim)]) for position in (source, target)]
    chosen = jax.random.permutation(own_key, shards_of)[partner]
    strong = (owner == chosen) | (owner == (partner + shards_of // 2) % shards_of)
    return jnp.where(strong, factor * drawn, drawn)


def levels(own_key, shape, shards, low, top_value):
    loudness, own = 1.0, jax.random.fold_in(own_key, 6)
    for position, shards_of in shards:
        heights = jnp.exp(jax.random.uniform(jax.random.fold_in(own, position), (shards_of,), jnp.float32, low / len(shards), top_value / len(shards)))
        loudness = loudness * jnp.repeat(heights, shape[position] // shards_of).reshape([-1 if axis == position else 1 for axis in range(len(shape))])
    return loudness


def noise(rng, shape, width, bound, shards=(), held_as=jnp.bfloat16):
    drawn = jax.random.normal(rng, shape, jnp.float32) * width
    if len(shards) > 0:
        drawn = levels(rng, shape, shards, -0.22, 0.18) * drawn
    return jnp.clip(drawn, min=-bound, max=bound).astype(held_as)


def gaussian_with(key, dims, spread, bound, cuts, heavy, kind=jnp.bfloat16):
    values = spread * jax.random.normal(key, dims, jnp.float32)
    if cuts:
        values = values * levels(key, dims, cuts, -0.22, 0.18)
    return jnp.clip(raised(values, jax.random.fold_in(key, 3), *heavy), -bound, bound).astype(kind)


def setup_inputs(seed: int = 0) -> dict:
    key_list = jax.random.split(jax.random.key(seed), 5)
    acts = gaussian_with(key_list[0], (BLOCKS, TOKENS, BW), 1.0, 6.0, ((0, 4), (1, 8)), (1, 2, 8, 2.0))
    factor_old = draw_factor_old(jax.random.fold_in(key_list[4], 71), 0)
    basis_old = noise(key_list[2], (BLOCKS, BW, RANK), BW ** -0.5, 0.09375, ((0, 4), (1, 8)))
    grads = gaussian_with(key_list[3], (BLOCKS, BW, OUTW), 2.0, 12.0, ((1, 8), (2, 4)), (1, 2, 8, 2.0))
    return dict(acts=acts, factor_old=factor_old, basis_old=basis_old, grads=grads)


def one_block(inputs):
    acts_b, factor_b, basis_b, grad_b = inputs
    projected = jnp.dot(acts_b.astype(jnp.float32), basis_b.astype(jnp.float32), preferred_element_type=jnp.float32).astype(jnp.bfloat16)
    token_sum = lax.dot_general(acts_b.astype(jnp.float32), projected.astype(jnp.float32), (((0,), (0,)), ((), ())), preferred_element_type=jnp.float32)
    applied = 0.25 * jnp.dot(factor_b.astype(jnp.float32), basis_b.astype(jnp.float32), preferred_element_type=jnp.float32) + 0.75 / TOKENS * token_sum
    applied_rows = applied * math.sqrt(BW)
    gram = jnp.dot(applied.T, applied, precision=lax.Precision.HIGHEST)
    lower = jnp.linalg.cholesky(gram)
    eigen_vals = jnp.diagonal(lower).astype(jnp.bfloat16)
    solved = lax.linalg.triangular_solve(lower, applied, left_side=False, lower=True, transpose_a=True)
    fresh = solved.astype(jnp.bfloat16)
    coupling = lax.dot_general(fresh.astype(jnp.float32), grad_b.astype(jnp.float32), (((0,), (0,)), ((), ())), preferred_element_type=jnp.float32)
    factors = 1.0 / (eigen_vals.astype(jnp.float32) + 2.0) - 0.5
    scaled = (factors[:, None] * coupling).astype(jnp.bfloat16)
    result = grad_b.astype(jnp.float32) * 0.5 + jnp.dot(fresh.astype(jnp.float32), scaled.astype(jnp.float32), preferred_element_type=jnp.float32)
    return (fresh, eigen_vals, result.astype(jnp.bfloat16), applied_rows)

def reference(acts, factor_old, basis_old, grads):
    fresh, eigen_vals, result, applied_rows = lax.map(one_block, (acts, factor_old, basis_old, grads))
    return (fresh, eigen_vals, result, applied_rows)
```

```python
import functools
import math

import jax
import jax.numpy as jnp
from jax import lax
from jax.experimental import pallas as pl
from jax.experimental.pallas import tpu as pltpu
from jax.sharding import PartitionSpec as P

decay_rate = 0.25
damping = 2.0
PANEL = 32
HIGHEST = lax.Precision.HIGHEST
F32 = jnp.float32
BF16 = jnp.bfloat16


def loop(count, body):
    if count <= 4:
        for i in range(count):
            body(i)
    elif count > 0:

        def step(i, carry):
            body(i)
            return carry

        lax.fori_loop(0, count, step, 0)


def dot_nn(a, b, **kw):
    return lax.dot_general(a, b, (((1,), (0,)), ((), ())), preferred_element_type=F32, **kw)


def dot_tn(a, b, **kw):
    return lax.dot_general(a, b, (((0,), (0,)), ((), ())), preferred_element_type=F32, **kw)


def dot_nt(a, b, **kw):
    return lax.dot_general(a, b, (((1,), (1,)), ((), ())), preferred_element_type=F32, **kw)


def pieces(value):
    high = value.astype(BF16)
    rest = value - high.astype(F32)
    mid = rest.astype(BF16)
    return high, mid, (rest - mid.astype(F32)).astype(BF16)


def narrow_nn(a, b):
    ah, am, al = pieces(a)
    bh, bm, bl = pieces(b)
    return dot_nn(
        jnp.concatenate([ah, ah, am, ah, al, am], axis=1),
        jnp.concatenate([bh, bm, bh, bl, bh, bm], axis=0),
    )


def narrow_nt(a, b):
    ah, am, al = pieces(a)
    bh, bm, bl = pieces(b)
    return dot_nt(
        jnp.concatenate([ah, ah, am, ah, al, am], axis=1),
        jnp.concatenate([bh, bm, bh, bl, bh, bm], axis=1),
    )


def panel_factor(block, n):
    rows = lax.broadcasted_iota(jnp.int32, (n, n), 0)
    cols = lax.broadcasted_iota(jnp.int32, (n, n), 1)
    x = jnp.concatenate([block, (rows == cols).astype(F32)], axis=1)
    tile = (8, 2 * n)
    row = lax.broadcasted_iota(jnp.int32, tile, 0)
    tiles = [x[t : t + 8, :] for t in range(0, n, 8)]
    pivots = [jnp.ones(tile, F32) for _ in tiles]
    for j in range(0, n, 4):
        own, sub = j // 8, j % 8
        live = range(own, n // 8)
        c = [{t: jnp.broadcast_to(tiles[t][:, j + m : j + m + 1], tile) for t in live} for m in range(4)]
        r = [jnp.broadcast_to(tiles[own][sub + m : sub + m + 1, :], tile) for m in range(4)]
        p = {
            (i, m): jnp.broadcast_to(c[m][own][sub + i : sub + i + 1, :], tile)
            for m in range(4)
            for i in range(m, 4)
        }
        change = {t: None for t in live}
        for m in range(4):
            pivots[own] = jnp.where(row == sub + m, p[m, m], pivots[own])
            inv = 1.0 / p[m, m]
            scaled = r[m] * inv
            for t in live:
                column = jnp.where(row > sub + m, c[m][t], 0.0) if t == own else c[m][t]
                change[t] = column * scaled if change[t] is None else change[t] + column * scaled
            for i in range(m + 1, 4):
                f = p[i, m] * inv
                for q in range(m + 1, i + 1):
                    p[i, q] = p[i, q] - f * p[q, m]
                r[i] = r[i] - f * r[m]
                for t in live:
                    c[i][t] = c[i][t] - f * c[m][t]
        for t in live:
            tiles[t] = tiles[t] - change[t]
    root = [jnp.sqrt(d) for d in pivots]
    inverse = jnp.concatenate([t / d for t, d in zip(tiles, root)], axis=0)[:, n:]
    return jnp.concatenate(root, axis=0)[:, :1], inverse


def cholesky_step(k, found, aug, roots, done):
    order, width = aug.shape
    root, inverse = found
    here = pl.ds(pl.multiple_of(k * PANEL, PANEL), PANEL)
    after = jnp.minimum(k + 1, order // PANEL - 1)
    below = pl.ds(pl.multiple_of(after * PANEL, PANEL), PANEL)
    roots[here, :] = root
    mine = aug[here, :]
    next_rows = aug[below, : 2 * PANEL]
    next_left = narrow_nt(next_rows[:, :PANEL], inverse)
    next_strip = narrow_nn(inverse, mine[:, PANEL : 2 * PANEL])
    ahead = panel_factor(next_rows[:, PANEL:] - narrow_nn(next_left, next_strip), PANEL)
    strip = narrow_nn(inverse, mine)
    lower = lax.broadcasted_iota(jnp.int32, (order, 1), 0) >= (k + 1) * PANEL
    left = jnp.where(lower, narrow_nt(aug[:, :PANEL], inverse), 0.0)
    aug[...] = aug[...] - narrow_nn(left, strip)
    aug[here, :] = strip
    done(k, root, pltpu.roll(strip, width - order + k * PANEL, 1)[:, :order])
    aug[...] = pltpu.roll(aug[...], width - PANEL, 1)
    return ahead


def finish_kernel(
    mall, cfull, appall, grads, applied, new_basis, eigen, out, fresh, rows, eigen_out, *, scale
):
    rank = applied.shape[1]
    scaled = dot_nn(mall[0, :, 1].reshape(rank, rank), cfull[...].reshape(rank, cfull.shape[2])).astype(BF16)
    scaled = dot_tn(mall[0, :, 0].reshape(rank, rank), scaled).astype(BF16)
    out[0] = (grads[0].astype(F32) / damping + dot_nn(appall[0], scaled)).astype(BF16)

    @pl.when(pl.program_id(0) == 0)
    def _():
        fresh[...] = new_basis[...]
        rows[...] = applied[...] * scale
        eigen_out[...] = eigen[...].astype(BF16)


def kernel(
    layers, Z, Y, token_total,
    acts_hbm, factor_hbm, basis_hbm, grads_hbm,
    mall, cfull, appall, applied_ref, fresh_ref, eigen_ref,
    acts, factor, grads, qfull, projected, fq,
    ysend_a, ybuf_a, zsend_a, zbuf_a,
    gpart, gbuf, gfull, aug, roots,
    c0p, ysend_c, ybuf_c, zsend_c, zbuf_c,
    load_sem,
    ag_z, ag_y, ag_zf, ag_yf, ag_recv,
    ys_a, yr_a, zs_a, zr_a,
    lay_send, lay_recv,
    gs_send, gs_recv, gg_send, gg_recv,
    ys_c, yr_c, zs_c, zr_c,
    cg_z, cg_y, cg_zf, cg_yf, cg_recv,
    m_send, m_recv,
):
    ag = (ag_z, ag_y, ag_zf, ag_yf, ag_recv)
    cg = (cg_z, cg_y, cg_zf, cg_yf, cg_recv)
    layer = lax.axis_index("layer")
    me = lax.axis_index("dp")
    z, y = me // Y, me % Y
    dp = Z * Y
    rows = factor.shape[0]
    rank = qfull.shape[2]
    zorder = [2, 1, 3] if Z == 4 else list(range(1, Z))

    def zpeer(k):
        return lax.rem(z + k, Z)

    def ypeer(j):
        return lax.rem(y + j, Y)

    def send(src, dst, ssem, rsem, **where):
        return pltpu.make_async_remote_copy(
            src_ref=src, dst_ref=dst, send_sem=ssem, recv_sem=rsem,
            device_id=where, device_id_type=pl.DeviceIdType.MESH,
        )

    loads = [
        pltpu.make_async_copy(src, dst, load_sem.at[i])
        for i, (src, dst) in enumerate(
            [
                (basis_hbm.at[0], qfull.at[me]),
                (acts_hbm.at[0], acts),
                (factor_hbm.at[0], factor),
                (grads_hbm, grads),
            ]
        )
    ]
    for load in loads:
        load.start()

    barrier = pltpu.get_barrier_semaphore()

    def greet_dp(i):
        pl.semaphore_signal(
            barrier, inc=1, device_id={"dp": lax.rem(me + 1 + i, dp)}, device_id_type=pl.DeviceIdType.MESH
        )

    def greet_layer(i):
        pl.semaphore_signal(
            barrier, inc=1, device_id={"layer": lax.rem(layer + 1 + i, layers)}, device_id_type=pl.DeviceIdType.MESH
        )

    loop(dp - 1, greet_dp)
    loop(layers - 1, greet_layer)
    pl.semaphore_wait(barrier, dp - 1 + layers - 1)

    def arrived(full, s, sems):
        send(full.at[s], full.at[s], sems[0].at[0], sems[4].at[s], dp=lax.rem(me + 1, dp)).wait_recv()

    def own_sends(full, sems, act):
        for i, side in enumerate((-1, 1)):
            @pl.when((z + side >= 0) & (z + side < Z))
            def _():
                act(send(full.at[me], full.at[me], sems[0].at[i], sems[4].at[me], dp=(z + side) * Y + y))

        def to_y(j):
            act(send(full.at[me], full.at[me], sems[1].at[j], sems[4].at[me], dp=z * Y + ypeer(j + 1)))

        loop(Y - 1, to_y)

    def passed_on(full, sems, dist, act, before=None, after=None):
        for i, side in enumerate((-1, 1)):
            @pl.when((z + side * dist >= 0) & (z + side * dist < Z))
            def _():
                s = (z + side * dist) * Y + y
                if before is not None:
                    before(s)

                @pl.when((z - side >= 0) & (z - side < Z))
                def _():
                    act(
                        send(
                            full.at[s], full.at[s], sems[2].at[i, dist - 1], sems[4].at[s], dp=(z - side) * Y + y
                        )
                    )

                def forward(j):
                    act(
                        send(
                            full.at[s], full.at[s], sems[3].at[i, dist - 1, j], sems[4].at[s],
                            dp=z * Y + ypeer(j + 1),
                        )
                    )

                loop(Y - 1, forward)
                if after is not None:
                    after(s)

    def gather_start(full, sems):
        own_sends(full, sems, lambda copy: copy.start())

    def gather_stage(full, sems, dist, use=None):
        passed_on(full, sems, dist, lambda copy: copy.start(), lambda s: arrived(full, s, sems), use)

    def gather_rows(full, sems, use):
        def take_row(zs):
            def take(j):
                s = zs * Y + ypeer(j + 1)
                arrived(full, s, sems)
                use(s)

            loop(Y - 1, take)

        take_row(z)
        for dist in range(1, Z):
            for side in (-1, 1):
                @pl.when((z + side * dist >= 0) & (z + side * dist < Z))
                def _():
                    take_row(z + side * dist)

    def gather_done(full, sems):
        own_sends(full, sems, lambda copy: copy.wait_send())
        for dist in range(1, Z):
            passed_on(full, sems, dist, lambda copy: copy.wait_send())

    korder = zorder + [0]

    def y_copy(k, j, ysend, ybuf, ys, yr):
        return send(
            ysend.at[k, j], ybuf.at[k, j], ys.at[k, j], yr.at[k, j], dp=z * Y + ypeer(j + 1)
        )

    def z_copy(k, zsend, zbuf, zs, zr):
        return send(zsend.at[k - 1], zbuf.at[k - 1], zs.at[k - 1], zr.at[k - 1], dp=zpeer(k) * Y + y)

    def scatter_y(produce, ysend, ybuf, ys, yr):
        for k in korder:

            def body(j):
                ysend[k, j] = produce(zpeer(k) * Y + ypeer(j + 1)).astype(BF16)
                y_copy(k, j, ysend, ybuf, ys, yr).start()

            loop(Y - 1, body)

    def scatter_z(produce, ysend, ybuf, ys, yr, zsend, zbuf, zs, zr):
        total = None
        for k in korder:
            total = produce(zpeer(k) * Y + y)
            for j in range(Y - 1):
                y_copy(k, j, ysend, ybuf, ys, yr).wait_recv()
                total = total + ybuf[k, j].astype(F32)
            if k > 0:
                zsend[k - 1] = total.astype(BF16)
                z_copy(k, zsend, zbuf, zs, zr).start()
        return total

    def scatter_sum(total, zsend, zbuf, zs, zr):
        for k in range(1, Z):
            z_copy(k, zsend, zbuf, zs, zr).wait_recv()
            total = total + zbuf[k - 1].astype(F32)
        return total

    def scatter_done(ysend, ybuf, ys, yr, zsend, zbuf, zs, zr):
        for k in range(Z):
            loop(Y - 1, lambda j: y_copy(k, j, ysend, ybuf, ys, yr).wait_send())
        for k in range(1, Z):
            z_copy(k, zsend, zbuf, zs, zr).wait_send()

    loads[0].wait()
    gather_start(qfull, ag)
    loads[1].wait()
    loads[2].wait()

    def columns(s):
        return pl.ds(pl.multiple_of(s * rows, rows), rows)

    def use_basis(s):
        block = qfull[s]
        projected[...] += dot_nn(acts[:, columns(s)], block)
        fq[...] += dot_nn(factor[:, columns(s)], block)

    own = qfull[me]
    projected[...] = dot_nn(acts[:, columns(me)], own)
    fq[...] = dot_nn(factor[:, columns(me)], own)
    for dist in range(1, Z):
        gather_stage(qfull, ag, dist, use_basis)
    gather_rows(qfull, ag, use_basis)

    short = projected[...].astype(BF16)

    def token_part(s):
        return dot_tn(acts[:, columns(s)], short)

    scatter_y(token_part, ysend_a, ybuf_a, ys_a, yr_a)
    total = scatter_z(token_part, ysend_a, ybuf_a, ys_a, yr_a, zsend_a, zbuf_a, zs_a, zr_a)
    total = scatter_sum(total, zsend_a, zbuf_a, zs_a, zr_a)
    applied = decay_rate * fq[...] + (1.0 - decay_rate) / token_total * total
    applied_ref[...] = applied
    appall[layer] = applied.astype(BF16)

    pair, core = layer // 2, layer % 2
    pairs = layers // 2
    partner = pair * 2 + 1 - core

    def same_core(i):
        return lax.rem(pair + 1 + i, pairs) * 2 + core

    def layer_own(act):
        act(send(appall.at[layer], appall.at[layer], lay_send.at[pairs - 1], lay_recv.at[layer], layer=partner))

        def out(i):
            act(send(appall.at[layer], appall.at[layer], lay_send.at[i], lay_recv.at[layer], layer=same_core(i)))

        loop(pairs - 1, out)

    def layer_pass(i, act):
        b = same_core(i)
        act(send(appall.at[b], appall.at[b], lay_send.at[pairs + i], lay_recv.at[b], layer=partner))

    def layer_wait(b):
        send(appall.at[b], appall.at[b], lay_send.at[0], lay_recv.at[b], layer=partner).wait_recv()

    layer_own(lambda copy: copy.start())

    gpart[...] = dot_tn(applied, applied, precision=HIGHEST)
    strip = rank // dp

    def strip_of(s):
        return pl.ds(pl.multiple_of(s * strip, strip), strip)

    def strip_copy(i):
        to = lax.rem(me + 1 + i, dp)
        return send(gpart.at[strip_of(to)], gbuf.at[me], gs_send.at[i], gs_recv.at[me], dp=to)

    loop(dp - 1, lambda i: strip_copy(i).start())

    chunk = cfull.shape[1]
    per = rank // chunk

    def coupling_chunk(s):
        return c0p[pl.ds(pl.multiple_of(s * chunk, chunk), chunk), :]

    def coupling_part(b):
        c0p[pl.ds(pl.multiple_of(b * rank, rank), rank), :] = dot_tn(appall[b], grads[b])
        for i in range(per):
            s = b * per + i
            k = lax.rem(s // Y - z + Z, Z)
            j = lax.rem(s % Y - y + Y, Y) - 1

            @pl.when(j >= 0)
            def _():
                ysend_c[k, j] = coupling_chunk(s).astype(BF16)
                y_copy(k, j, ysend_c, ybuf_c, ys_c, yr_c).start()

    loads[3].wait()
    coupling_part(layer)
    layer_wait(partner)
    coupling_part(partner)
    gbuf[me] = gpart[strip_of(me), :]

    def strip_wait(i):
        s = lax.rem(me + 1 + i, dp)
        send(gpart.at[strip_of(s)], gbuf.at[s], gs_send.at[i], gs_recv.at[s], dp=s).wait_recv()

    loop(dp - 1, strip_wait)
    summed = gbuf[0]
    for s in range(1, dp):
        summed = summed + gbuf[s]
    gfull[strip_of(me), :] = summed

    def full_copy(i):
        to = lax.rem(me + 1 + i, dp)
        return send(gfull.at[strip_of(me)], gfull.at[strip_of(me)], gg_send.at[i], gg_recv.at[me], dp=to)

    loop(dp - 1, lambda i: full_copy(i).start())

    def other_chip(i):
        b = same_core(i)
        layer_wait(b)
        layer_pass(i, lambda copy: copy.start())
        coupling_part(b)

    def other_chip_core(i):
        b = lax.rem(pair + 1 + i, pairs) * 2 + 1 - core
        layer_wait(b)
        coupling_part(b)

    loop(pairs - 1, other_chip)
    loop(pairs - 1, other_chip_core)

    def full_wait(i):
        s = lax.rem(me + 1 + i, dp)
        send(
            gfull.at[strip_of(s)], gfull.at[strip_of(s)], gg_send.at[i], gg_recv.at[s], dp=s
        ).wait_recv()

    loop(dp - 1, full_wait)
    aug[:, :rank] = gfull[...]
    aug[:, rank:] = (
        lax.broadcasted_iota(jnp.int32, (rank, rank), 0) == lax.broadcasted_iota(jnp.int32, (rank, rank), 1)
    ).astype(F32)

    panels = rank // PANEL

    def m_copy(k, i):
        return send(
            mall.at[layer, k], mall.at[layer, k], m_send.at[k, i], m_recv.at[layer, k],
            layer=lax.rem(layer + 1 + i, layers),
        )

    def rows_done(k, root, finished):
        factors = 1.0 / (root.astype(BF16).astype(F32) + damping) - 1.0 / damping
        mall[layer, k, 0] = finished.astype(BF16)
        mall[layer, k, 1] = (factors * finished).astype(BF16)
        loop(layers - 1, lambda i: m_copy(k, i).start())

    def factor_panels(first, last, found):
        return lax.fori_loop(first, last, lambda k, at: cholesky_step(k, at, aug, roots, rows_done), found)

    found = panel_factor(aug[:PANEL, :PANEL], PANEL)
    found = factor_panels(0, (panels - Z + 2) // 2, found)
    total = scatter_z(coupling_chunk, ysend_c, ybuf_c, ys_c, yr_c, zsend_c, zbuf_c, zs_c, zr_c)
    found = factor_panels((panels - Z + 2) // 2, panels - Z + 1, found)
    total = scatter_sum(total, zsend_c, zbuf_c, zs_c, zr_c)
    cfull[me] = total.astype(BF16)
    gather_start(cfull, cg)
    for dist in range(1, Z):
        found = factor_panels(panels - Z + dist, panels - Z + dist + 1, found)
        gather_stage(cfull, cg, dist)

    inverse = aug[:, :rank]
    eigen = roots[...].astype(BF16)
    on_diagonal = lax.broadcasted_iota(jnp.int32, (rank, rank), 0) == lax.broadcasted_iota(
        jnp.int32, (rank, rank), 1
    )
    eigen_ref[...] = jnp.sum(jnp.where(on_diagonal, eigen.astype(F32), 0.0), axis=0, keepdims=True)
    fresh_ref[...] = dot_nt(applied_ref[...], inverse, precision=HIGHEST).astype(BF16)
    gather_rows(cfull, cg, lambda s: None)

    def m_wait(i):
        b = lax.rem(layer + 1 + i, layers)
        for k in range(panels):
            send(mall.at[b, k], mall.at[b, k], m_send.at[k, i], m_recv.at[b, k], layer=b).wait_recv()

    loop(layers - 1, m_wait)

    gather_done(qfull, ag)
    scatter_done(ysend_a, ybuf_a, ys_a, yr_a, zsend_a, zbuf_a, zs_a, zr_a)
    layer_own(lambda copy: copy.wait_send())
    loop(pairs - 1, lambda i: layer_pass(i, lambda copy: copy.wait_send()))
    loop(dp - 1, lambda i: strip_copy(i).wait_send())
    loop(dp - 1, lambda i: full_copy(i).wait_send())
    scatter_done(ysend_c, ybuf_c, ys_c, yr_c, zsend_c, zbuf_c, zs_c, zr_c)
    gather_done(cfull, cg)
    for k in range(panels):
        loop(layers - 1, lambda i: m_copy(k, i).wait_send())


def per_device(layers, dp, acts, factor_old, basis_old, grads):
    Z = 4 if dp % 4 == 0 else 1
    Y = dp // Z
    tokens, width = acts.shape[1:]
    rows, rank = basis_old.shape[1:]
    blocks, _, cols = grads.shape
    chunk = blocks * rank // dp
    V, DMA = pltpu.VMEM, pltpu.SemaphoreType.DMA
    Y1, Z1, L1 = max(Y - 1, 1), max(Z - 1, 1), max(layers - 1, 1)
    scratch = [
        V((tokens, width), BF16),
        V((rows, width), BF16),
        V((blocks, rows, cols), BF16),
        V((dp, rows, rank), BF16),
        V((tokens, rank), F32),
        V((rows, rank), F32),
        V((Z, Y1, rows, rank), BF16),
        V((Z, Y1, rows, rank), BF16),
        V((Z1, rows, rank), BF16),
        V((Z1, rows, rank), BF16),
        V((rank, rank), F32),
        V((dp, rank // dp, rank), F32),
        V((rank, rank), F32),
        V((rank, 2 * rank), F32),
        V((rank, 1), F32),
        V((blocks * rank, cols), F32),
        V((Z, Y1, chunk, cols), BF16),
        V((Z, Y1, chunk, cols), BF16),
        V((Z1, chunk, cols), BF16),
        V((Z1, chunk, cols), BF16),
        DMA((4,)),
        DMA((2,)), DMA((Y1,)), DMA((2, Z1)), DMA((2, Z1, Y1)), DMA((dp,)),
        DMA((Z, Y1)), DMA((Z, Y1)), DMA((Z1,)), DMA((Z1,)),
        DMA((L1,)), DMA((layers,)),
        DMA((dp,)), DMA((dp,)), DMA((dp,)), DMA((dp,)),
        DMA((Z, Y1)), DMA((Z, Y1)), DMA((Z1,)), DMA((Z1,)),
        DMA((2,)), DMA((Y1,)), DMA((2, Z1)), DMA((2, Z1, Y1)), DMA((dp,)),
        DMA((rank // PANEL, L1)), DMA((layers, rank // PANEL)),
    ]
    vmem = pl.BlockSpec(memory_space=pltpu.VMEM)
    mall, cfull, appall, applied, new_basis, eigen = pl.pallas_call(
        functools.partial(kernel, layers, Z, Y, tokens * dp),
        out_shape=(
            jax.ShapeDtypeStruct((blocks, rank // PANEL, 2, PANEL, rank), BF16),
            jax.ShapeDtypeStruct((dp, chunk, cols), BF16),
            jax.ShapeDtypeStruct((blocks, rows, rank), BF16),
            jax.ShapeDtypeStruct((rows, rank), F32),
            jax.ShapeDtypeStruct((rows, rank), BF16),
            jax.ShapeDtypeStruct((1, rank), F32),
        ),
        in_specs=[pl.BlockSpec(memory_space=pltpu.HBM)] * 4,
        out_specs=(vmem,) * 6,
        scratch_shapes=scratch,
        compiler_params=pltpu.CompilerParams(
            collective_id=0, has_side_effects=True, vmem_limit_bytes=50 * 1024 * 1024
        ),
    )(acts, factor_old, basis_old, grads)
    per = rank // chunk
    by_block = lambda b: (b, 0, 0)
    whole = lambda b: (0, 0)
    conditioned, fresh, applied_rows, eigen = pl.pallas_call(
        functools.partial(finish_kernel, scale=math.sqrt(width)),
        grid=(blocks,),
        out_shape=(
            jax.ShapeDtypeStruct((blocks, rows, cols), BF16),
            jax.ShapeDtypeStruct((rows, rank), BF16),
            jax.ShapeDtypeStruct((rows, rank), F32),
            jax.ShapeDtypeStruct((1, rank), BF16),
        ),
        in_specs=[
            pl.BlockSpec((1, rank // PANEL, 2, PANEL, rank), lambda b: (b, 0, 0, 0, 0)),
            pl.BlockSpec((per, chunk, cols), by_block),
            pl.BlockSpec((1, rows, rank), by_block),
            pl.BlockSpec((1, rows, cols), by_block),
            pl.BlockSpec((rows, rank), whole),
            pl.BlockSpec((rows, rank), whole),
            pl.BlockSpec((1, rank), whole),
        ],
        out_specs=(
            pl.BlockSpec((1, rows, cols), by_block),
            pl.BlockSpec((rows, rank), whole),
            pl.BlockSpec((rows, rank), whole),
            pl.BlockSpec((1, rank), whole),
        ),
        compiler_params=pltpu.CompilerParams(vmem_limit_bytes=12 * 1024 * 1024),
    )(mall, cfull, appall, grads, applied, new_basis, eigen)
    return fresh[None], eigen, conditioned, applied_rows[None]


def solution(mesh):
    in_specs = (
        P("layer", "dp", None),
        P("layer", "dp", None),
        P("layer", "dp", None),
        P(None, "dp", "layer"),
    )
    out_specs = (
        P("layer", "dp", None),
        P("layer", None),
        P(None, "dp", "layer"),
        P("layer", "dp", None),
    )
    body = functools.partial(per_device, mesh.shape["layer"], mesh.shape["dp"])
    return jax.shard_map(body, mesh=mesh, in_specs=in_specs, out_specs=out_specs, check_vma=False)
```

```python
import functools
import math

import jax
import jax.numpy as jnp
from jax import lax
from jax.experimental import pallas as pl
from jax.experimental.pallas import tpu as pltpu
from jax.sharding import PartitionSpec as P

decay_rate = 0.25
damping = 2.0
PANEL = 32
HIGHEST = lax.Precision.HIGHEST
F32 = jnp.float32
BF16 = jnp.bfloat16


def loop(count, body):
    if count <= 4:
        for i in range(count):
            body(i)
    elif count > 0:

        def step(i, carry):
            body(i)
            return carry

        lax.fori_loop(0, count, step, 0)


def dot_nn(a, b, **kw):
    return lax.dot_general(a, b, (((1,), (0,)), ((), ())), preferred_element_type=F32, **kw)


def dot_tn(a, b, **kw):
    return lax.dot_general(a, b, (((0,), (0,)), ((), ())), preferred_element_type=F32, **kw)


def dot_nt(a, b, **kw):
    return lax.dot_general(a, b, (((1,), (1,)), ((), ())), preferred_element_type=F32, **kw)


def pieces(value):
    high = value.astype(BF16)
    rest = value - high.astype(F32)
    mid = rest.astype(BF16)
    return high, mid, (rest - mid.astype(F32)).astype(BF16)


def narrow_nn(a, b):
    ah, am, al = pieces(a)
    bh, bm, bl = pieces(b)
    return dot_nn(
        jnp.concatenate([ah, ah, am, ah, al, am], axis=1),
        jnp.concatenate([bh, bm, bh, bl, bh, bm], axis=0),
    )


def narrow_nt(a, b):
    ah, am, al = pieces(a)
    bh, bm, bl = pieces(b)
    return dot_nt(
        jnp.concatenate([ah, ah, am, ah, al, am], axis=1),
        jnp.concatenate([bh, bm, bh, bl, bh, bm], axis=1),
    )


def panel_factor(block, n):
    rows = lax.broadcasted_iota(jnp.int32, (n, n), 0)
    cols = lax.broadcasted_iota(jnp.int32, (n, n), 1)
    x = jnp.concatenate([block, (rows == cols).astype(F32)], axis=1)
    tile = (8, 2 * n)
    row = lax.broadcasted_iota(jnp.int32, tile, 0)
    tiles = [x[t : t + 8, :] for t in range(0, n, 8)]
    pivots = [jnp.ones(tile, F32) for _ in tiles]
    for j in range(0, n, 4):
        own, sub = j // 8, j % 8
        live = range(own, n // 8)
        c = [{t: jnp.broadcast_to(tiles[t][:, j + m : j + m + 1], tile) for t in live} for m in range(4)]
        r = [jnp.broadcast_to(tiles[own][sub + m : sub + m + 1, :], tile) for m in range(4)]
        p = {
            (i, m): jnp.broadcast_to(c[m][own][sub + i : sub + i + 1, :], tile)
            for m in range(4)
            for i in range(m, 4)
        }
        change = {t: None for t in live}
        for m in range(4):
            pivots[own] = jnp.where(row == sub + m, p[m, m], pivots[own])
            inv = 1.0 / p[m, m]
            scaled = r[m] * inv
            for t in live:
                column = jnp.where(row > sub + m, c[m][t], 0.0) if t == own else c[m][t]
                change[t] = column * scaled if change[t] is None else change[t] + column * scaled
            for i in range(m + 1, 4):
                f = p[i, m] * inv
                for q in range(m + 1, i + 1):
                    p[i, q] = p[i, q] - f * p[q, m]
                r[i] = r[i] - f * r[m]
                for t in live:
                    c[i][t] = c[i][t] - f * c[m][t]
        for t in live:
            tiles[t] = tiles[t] - change[t]
    root = [jnp.sqrt(d) for d in pivots]
    inverse = jnp.concatenate([t / d for t, d in zip(tiles, root)], axis=0)[:, n:]
    return jnp.concatenate(root, axis=0)[:, :1], inverse


def cholesky_step(k, found, aug, roots, done):
    order, width = aug.shape
    root, inverse = found
    here = pl.ds(pl.multiple_of(k * PANEL, PANEL), PANEL)
    after = jnp.minimum(k + 1, order // PANEL - 1)
    below = pl.ds(pl.multiple_of(after * PANEL, PANEL), PANEL)
    roots[here, :] = root
    mine = aug[here, :]
    next_rows = aug[below, : 2 * PANEL]
    next_left = narrow_nt(next_rows[:, :PANEL], inverse)
    next_strip = narrow_nn(inverse, mine[:, PANEL : 2 * PANEL])
    ahead = panel_factor(next_rows[:, PANEL:] - narrow_nn(next_left, next_strip), PANEL)
    strip = narrow_nn(inverse, mine)
    lower = lax.broadcasted_iota(jnp.int32, (order, 1), 0) >= (k + 1) * PANEL
    left = jnp.where(lower, narrow_nt(aug[:, :PANEL], inverse), 0.0)
    aug[...] = aug[...] - narrow_nn(left, strip)
    aug[here, :] = strip
    done(k, root, pltpu.roll(strip, width - order + k * PANEL, 1)[:, :order])
    aug[...] = pltpu.roll(aug[...], width - PANEL, 1)
    return ahead


def finish_kernel(
    mall, cfull, appall, grads, applied, new_basis, eigen, out, fresh, rows, eigen_out, *, scale
):
    rank = applied.shape[1]
    scaled = dot_nn(mall[0, :, 1].reshape(rank, rank), cfull[...].reshape(rank, cfull.shape[2])).astype(BF16)
    scaled = dot_tn(mall[0, :, 0].reshape(rank, rank), scaled).astype(BF16)
    out[0] = (grads[0].astype(F32) / damping + dot_nn(appall[0], scaled)).astype(BF16)

    @pl.when(pl.program_id(0) == 0)
    def _():
        fresh[...] = new_basis[...]
        rows[...] = applied[...] * scale
        eigen_out[...] = eigen[...].astype(BF16)


def kernel(
    layers, Z, Y, token_total,
    acts_hbm, factor_hbm, basis_hbm, grads_hbm,
    mall, cfull, appall, applied_ref, fresh_ref, eigen_ref,
    acts, factor, grads, qfull, projected, fq,
    ysend_a, ybuf_a, zsend_a, zbuf_a,
    gpart, gbuf, gfull, aug, roots,
    c0p, ysend_c, ybuf_c, zsend_c, zbuf_c,
    load_sem,
    ag_z, ag_y, ag_zf, ag_yf, ag_recv,
    ys_a, yr_a, zs_a, zr_a,
    lay_send, lay_recv,
    gs_send, gs_recv, gg_send, gg_recv,
    ys_c, yr_c, zs_c, zr_c,
    cg_z, cg_y, cg_zf, cg_yf, cg_recv,
    m_send, m_recv,
):
    ag = (ag_z, ag_y, ag_zf, ag_yf, ag_recv)
    cg = (cg_z, cg_y, cg_zf, cg_yf, cg_recv)
    layer = lax.axis_index("layer")
    me = lax.axis_index("dp")
    z, y = me // Y, me % Y
    dp = Z * Y
    rows = factor.shape[0]
    rank = qfull.shape[2]
    zorder = [2, 1, 3] if Z == 4 else list(range(1, Z))

    def zpeer(k):
        return lax.rem(z + k, Z)

    def ypeer(j):
        return lax.rem(y + j, Y)

    def send(src, dst, ssem, rsem, **where):
        return pltpu.make_async_remote_copy(
            src_ref=src, dst_ref=dst, send_sem=ssem, recv_sem=rsem,
            device_id=where, device_id_type=pl.DeviceIdType.MESH,
        )

    loads = [
        pltpu.make_async_copy(src, dst, load_sem.at[i])
        for i, (src, dst) in enumerate(
            [
                (basis_hbm.at[0], qfull.at[me]),
                (acts_hbm.at[0], acts),
                (factor_hbm.at[0], factor),
                (grads_hbm, grads),
            ]
        )
    ]
    for load in loads:
        load.start()

    barrier = pltpu.get_barrier_semaphore()

    def greet_dp(i):
        pl.semaphore_signal(
            barrier, inc=1, device_id={"dp": lax.rem(me + 1 + i, dp)}, device_id_type=pl.DeviceIdType.MESH
        )

    def greet_layer(i):
        pl.semaphore_signal(
            barrier, inc=1, device_id={"layer": lax.rem(layer + 1 + i, layers)}, device_id_type=pl.DeviceIdType.MESH
        )

    loop(dp - 1, greet_dp)
    loop(layers - 1, greet_layer)
    pl.semaphore_wait(barrier, dp - 1 + layers - 1)

    def arrived(full, s, sems):
        send(full.at[s], full.at[s], sems[0].at[0], sems[4].at[s], dp=lax.rem(me + 1, dp)).wait_recv()

    def own_sends(full, sems, act):
        for i, side in enumerate((-1, 1)):
            @pl.when((z + side >= 0) & (z + side < Z))
            def _():
                act(send(full.at[me], full.at[me], sems[0].at[i], sems[4].at[me], dp=(z + side) * Y + y))

        def to_y(j):
            act(send(full.at[me], full.at[me], sems[1].at[j], sems[4].at[me], dp=z * Y + ypeer(j + 1)))

        loop(Y - 1, to_y)

    def passed_on(full, sems, dist, act, before=None, after=None):
        for i, side in enumerate((-1, 1)):
            @pl.when((z + side * dist >= 0) & (z + side * dist < Z))
            def _():
                s = (z + side * dist) * Y + y
                if before is not None:
                    before(s)

                @pl.when((z - side >= 0) & (z - side < Z))
                def _():
                    act(
                        send(
                            full.at[s], full.at[s], sems[2].at[i, dist - 1], sems[4].at[s], dp=(z - side) * Y + y
                        )
                    )

                def forward(j):
                    act(
                        send(
                            full.at[s], full.at[s], sems[3].at[i, dist - 1, j], sems[4].at[s],
                            dp=z * Y + ypeer(j + 1),
                        )
                    )

                loop(Y - 1, forward)
                if after is not None:
                    after(s)

    def gather_start(full, sems):
        own_sends(full, sems, lambda copy: copy.start())

    def gather_stage(full, sems, dist, use=None):
        passed_on(full, sems, dist, lambda copy: copy.start(), lambda s: arrived(full, s, sems), use)

    def gather_rows(full, sems, use):
        def take_row(zs):
            def take(j):
                s = zs * Y + ypeer(j + 1)
                arrived(full, s, sems)
                use(s)

            loop(Y - 1, take)

        take_row(z)
        for dist in range(1, Z):
            for side in (-1, 1):
                @pl.when((z + side * dist >= 0) & (z + side * dist < Z))
                def _():
                    take_row(z + side * dist)

    def gather_done(full, sems):
        own_sends(full, sems, lambda copy: copy.wait_send())
        for dist in range(1, Z):
            passed_on(full, sems, dist, lambda copy: copy.wait_send())

    korder = zorder + [0]

    def y_copy(k, j, ysend, ybuf, ys, yr):
        return send(
            ysend.at[k, j], ybuf.at[k, j], ys.at[k, j], yr.at[k, j], dp=z * Y + ypeer(j + 1)
        )

    def z_copy(k, zsend, zbuf, zs, zr):
        return send(zsend.at[k - 1], zbuf.at[k - 1], zs.at[k - 1], zr.at[k - 1], dp=zpeer(k) * Y + y)

    def scatter_y(produce, ysend, ybuf, ys, yr):
        for k in korder:

            def body(j):
                ysend[k, j] = produce(zpeer(k) * Y + ypeer(j + 1)).astype(BF16)
                y_copy(k, j, ysend, ybuf, ys, yr).start()

            loop(Y - 1, body)

    def scatter_z(produce, ysend, ybuf, ys, yr, zsend, zbuf, zs, zr):
        total = None
        for k in korder:
            total = produce(zpeer(k) * Y + y)
            for j in range(Y - 1):
                y_copy(k, j, ysend, ybuf, ys, yr).wait_recv()
                total = total + ybuf[k, j].astype(F32)
            if k > 0:
                zsend[k - 1] = total.astype(BF16)
                z_copy(k, zsend, zbuf, zs, zr).start()
        return total

    def scatter_sum(total, zsend, zbuf, zs, zr):
        for k in range(1, Z):
            z_copy(k, zsend, zbuf, zs, zr).wait_recv()
            total = total + zbuf[k - 1].astype(F32)
        return total

    def scatter_done(ysend, ybuf, ys, yr, zsend, zbuf, zs, zr):
        for k in range(Z):
            loop(Y - 1, lambda j: y_copy(k, j, ysend, ybuf, ys, yr).wait_send())
        for k in range(1, Z):
            z_copy(k, zsend, zbuf, zs, zr).wait_send()

    loads[0].wait()
    gather_start(qfull, ag)
    loads[1].wait()
    loads[2].wait()

    def columns(s):
        return pl.ds(pl.multiple_of(s * rows, rows), rows)

    def use_basis(s):
        block = qfull[s]
        projected[...] += dot_nn(acts[:, columns(s)], block)
        fq[...] += dot_nn(factor[:, columns(s)], block)

    own = qfull[me]
    projected[...] = dot_nn(acts[:, columns(me)], own)
    fq[...] = dot_nn(factor[:, columns(me)], own)
    for dist in range(1, Z):
        gather_stage(qfull, ag, dist, use_basis)
    gather_rows(qfull, ag, use_basis)

    short = projected[...].astype(BF16)

    def token_part(s):
        return dot_tn(acts[:, columns(s)], short)

    scatter_y(token_part, ysend_a, ybuf_a, ys_a, yr_a)
    total = scatter_z(token_part, ysend_a, ybuf_a, ys_a, yr_a, zsend_a, zbuf_a, zs_a, zr_a)
    total = scatter_sum(total, zsend_a, zbuf_a, zs_a, zr_a)
    applied = decay_rate * fq[...] + (1.0 - decay_rate) / token_total * total
    applied_ref[...] = applied
    appall[layer] = applied.astype(BF16)

    pair, core = layer // 2, layer % 2
    pairs = layers // 2
    partner = pair * 2 + 1 - core

    def same_core(i):
        return lax.rem(pair + 1 + i, pairs) * 2 + core

    def layer_own(act):
        act(send(appall.at[layer], appall.at[layer], lay_send.at[pairs - 1], lay_recv.at[layer], layer=partner))

        def out(i):
            act(send(appall.at[layer], appall.at[layer], lay_send.at[i], lay_recv.at[layer], layer=same_core(i)))

        loop(pairs - 1, out)

    def layer_pass(i, act):
        b = same_core(i)
        act(send(appall.at[b], appall.at[b], lay_send.at[pairs + i], lay_recv.at[b], layer=partner))

    def layer_wait(b):
        send(appall.at[b], appall.at[b], lay_send.at[0], lay_recv.at[b], layer=partner).wait_recv()

    layer_own(lambda copy: copy.start())

    gpart[...] = dot_tn(applied, applied, precision=HIGHEST)
    strip = rank // dp

    def strip_of(s):
        return pl.ds(pl.multiple_of(s * strip, strip), strip)

    def strip_copy(i):
        to = lax.rem(me + 1 + i, dp)
        return send(gpart.at[strip_of(to)], gbuf.at[me], gs_send.at[i], gs_recv.at[me], dp=to)

    loop(dp - 1, lambda i: strip_copy(i).start())

    chunk = cfull.shape[1]
    per = rank // chunk

    def coupling_chunk(s):
        return c0p[pl.ds(pl.multiple_of(s * chunk, chunk), chunk), :]

    def coupling_part(b):
        c0p[pl.ds(pl.multiple_of(b * rank, rank), rank), :] = dot_tn(appall[b], grads[b])
        for i in range(per):
            s = b * per + i
            k = lax.rem(s // Y - z + Z, Z)
            j = lax.rem(s % Y - y + Y, Y) - 1

            @pl.when(j >= 0)
            def _():
                ysend_c[k, j] = coupling_chunk(s).astype(BF16)
                y_copy(k, j, ysend_c, ybuf_c, ys_c, yr_c).start()

    loads[3].wait()
    coupling_part(layer)
    layer_wait(partner)
    coupling_part(partner)
    gbuf[me] = gpart[strip_of(me), :]

    def strip_wait(i):
        s = lax.rem(me + 1 + i, dp)
        send(gpart.at[strip_of(s)], gbuf.at[s], gs_send.at[i], gs_recv.at[s], dp=s).wait_recv()

    loop(dp - 1, strip_wait)
    summed = gbuf[0]
    for s in range(1, dp):
        summed = summed + gbuf[s]
    gfull[strip_of(me), :] = summed

    def full_copy(i):
        to = lax.rem(me + 1 + i, dp)
        return send(gfull.at[strip_of(me)], gfull.at[strip_of(me)], gg_send.at[i], gg_recv.at[me], dp=to)

    loop(dp - 1, lambda i: full_copy(i).start())

    def other_chip(i):
        b = same_core(i)
        layer_wait(b)
        layer_pass(i, lambda copy: copy.start())
        coupling_part(b)

    def other_chip_core(i):
        b = lax.rem(pair + 1 + i, pairs) * 2 + 1 - core
        layer_wait(b)
        coupling_part(b)

    loop(pairs - 1, other_chip)
    loop(pairs - 1, other_chip_core)

    total = scatter_z(coupling_chunk, ysend_c, ybuf_c, ys_c, yr_c, zsend_c, zbuf_c, zs_c, zr_c)

    def full_wait(i):
        s = lax.rem(me + 1 + i, dp)
        send(
            gfull.at[strip_of(s)], gfull.at[strip_of(s)], gg_send.at[i], gg_recv.at[s], dp=s
        ).wait_recv()

    loop(dp - 1, full_wait)
    aug[:, :rank] = gfull[...]
    aug[:, rank:] = (
        lax.broadcasted_iota(jnp.int32, (rank, rank), 0) == lax.broadcasted_iota(jnp.int32, (rank, rank), 1)
    ).astype(F32)

    panels = rank // PANEL

    def m_copy(k, i):
        return send(
            mall.at[layer, k], mall.at[layer, k], m_send.at[k, i], m_recv.at[layer, k],
            layer=lax.rem(layer + 1 + i, layers),
        )

    def rows_done(k, root, finished):
        factors = 1.0 / (root.astype(BF16).astype(F32) + damping) - 1.0 / damping
        mall[layer, k, 0] = finished.astype(BF16)
        mall[layer, k, 1] = (factors * finished).astype(BF16)
        loop(layers - 1, lambda i: m_copy(k, i).start())

    def factor_panels(first, last, found):
        return lax.fori_loop(first, last, lambda k, at: cholesky_step(k, at, aug, roots, rows_done), found)

    found = panel_factor(aug[:PANEL, :PANEL], PANEL)
    found = factor_panels(0, 1, found)
    total = scatter_sum(total, zsend_c, zbuf_c, zs_c, zr_c)
    cfull[me] = total.astype(BF16)
    gather_start(cfull, cg)
    for dist in range(1, Z):
        found = factor_panels(dist, dist + 1, found)
        gather_stage(cfull, cg, dist)
    found = factor_panels(Z, panels, found)

    inverse = aug[:, :rank]
    eigen = roots[...].astype(BF16)
    on_diagonal = lax.broadcasted_iota(jnp.int32, (rank, rank), 0) == lax.broadcasted_iota(
        jnp.int32, (rank, rank), 1
    )
    eigen_ref[...] = jnp.sum(jnp.where(on_diagonal, eigen.astype(F32), 0.0), axis=0, keepdims=True)
    fresh_ref[...] = dot_nt(applied_ref[...], inverse, precision=HIGHEST).astype(BF16)
    gather_rows(cfull, cg, lambda s: None)

    def m_wait(i):
        b = lax.rem(layer + 1 + i, layers)
        for k in range(panels):
            send(mall.at[b, k], mall.at[b, k], m_send.at[k, i], m_recv.at[b, k], layer=b).wait_recv()

    loop(layers - 1, m_wait)

    gather_done(qfull, ag)
    scatter_done(ysend_a, ybuf_a, ys_a, yr_a, zsend_a, zbuf_a, zs_a, zr_a)
    layer_own(lambda copy: copy.wait_send())
    loop(pairs - 1, lambda i: layer_pass(i, lambda copy: copy.wait_send()))
    loop(dp - 1, lambda i: strip_copy(i).wait_send())
    loop(dp - 1, lambda i: full_copy(i).wait_send())
    scatter_done(ysend_c, ybuf_c, ys_c, yr_c, zsend_c, zbuf_c, zs_c, zr_c)
    gather_done(cfull, cg)
    for k in range(panels):
        loop(layers - 1, lambda i: m_copy(k, i).wait_send())


def per_device(layers, dp, acts, factor_old, basis_old, grads):
    Z = 4 if dp % 4 == 0 else 1
    Y = dp // Z
    tokens, width = acts.shape[1:]
    rows, rank = basis_old.shape[1:]
    blocks, _, cols = grads.shape
    chunk = blocks * rank // dp
    V, DMA = pltpu.VMEM, pltpu.SemaphoreType.DMA
    Y1, Z1, L1 = max(Y - 1, 1), max(Z - 1, 1), max(layers - 1, 1)
    scratch = [
        V((tokens, width), BF16),
        V((rows, width), BF16),
        V((blocks, rows, cols), BF16),
        V((dp, rows, rank), BF16),
        V((tokens, rank), F32),
        V((rows, rank), F32),
        V((Z, Y1, rows, rank), BF16),
        V((Z, Y1, rows, rank), BF16),
        V((Z1, rows, rank), BF16),
        V((Z1, rows, rank), BF16),
        V((rank, rank), F32),
        V((dp, rank // dp, rank), F32),
        V((rank, rank), F32),
        V((rank, 2 * rank), F32),
        V((rank, 1), F32),
        V((blocks * rank, cols), F32),
        V((Z, Y1, chunk, cols), BF16),
        V((Z, Y1, chunk, cols), BF16),
        V((Z1, chunk, cols), BF16),
        V((Z1, chunk, cols), BF16),
        DMA((4,)),
        DMA((2,)), DMA((Y1,)), DMA((2, Z1)), DMA((2, Z1, Y1)), DMA((dp,)),
        DMA((Z, Y1)), DMA((Z, Y1)), DMA((Z1,)), DMA((Z1,)),
        DMA((L1,)), DMA((layers,)),
        DMA((dp,)), DMA((dp,)), DMA((dp,)), DMA((dp,)),
        DMA((Z, Y1)), DMA((Z, Y1)), DMA((Z1,)), DMA((Z1,)),
        DMA((2,)), DMA((Y1,)), DMA((2, Z1)), DMA((2, Z1, Y1)), DMA((dp,)),
        DMA((rank // PANEL, L1)), DMA((layers, rank // PANEL)),
    ]
    vmem = pl.BlockSpec(memory_space=pltpu.VMEM)
    mall, cfull, appall, applied, new_basis, eigen = pl.pallas_call(
        functools.partial(kernel, layers, Z, Y, tokens * dp),
        out_shape=(
            jax.ShapeDtypeStruct((blocks, rank // PANEL, 2, PANEL, rank), BF16),
            jax.ShapeDtypeStruct((dp, chunk, cols), BF16),
            jax.ShapeDtypeStruct((blocks, rows, rank), BF16),
            jax.ShapeDtypeStruct((rows, rank), F32),
            jax.ShapeDtypeStruct((rows, rank), BF16),
            jax.ShapeDtypeStruct((1, rank), F32),
        ),
        in_specs=[pl.BlockSpec(memory_space=pltpu.HBM)] * 4,
        out_specs=(vmem,) * 6,
        scratch_shapes=scratch,
        compiler_params=pltpu.CompilerParams(
            collective_id=0, has_side_effects=True, vmem_limit_bytes=48 * 1024 * 1024
        ),
    )(acts, factor_old, basis_old, grads)
    per = rank // chunk
    by_block = lambda b: (b, 0, 0)
    whole = lambda b: (0, 0)
    conditioned, fresh, applied_rows, eigen = pl.pallas_call(
        functools.partial(finish_kernel, scale=math.sqrt(width)),
        grid=(blocks,),
        out_shape=(
            jax.ShapeDtypeStruct((blocks, rows, cols), BF16),
            jax.ShapeDtypeStruct((rows, rank), BF16),
            jax.ShapeDtypeStruct((rows, rank), F32),
            jax.ShapeDtypeStruct((1, rank), BF16),
        ),
        in_specs=[
            pl.BlockSpec((1, rank // PANEL, 2, PANEL, rank), lambda b: (b, 0, 0, 0, 0)),
            pl.BlockSpec((per, chunk, cols), by_block),
            pl.BlockSpec((1, rows, rank), by_block),
            pl.BlockSpec((1, rows, cols), by_block),
            pl.BlockSpec((rows, rank), whole),
            pl.BlockSpec((rows, rank), whole),
            pl.BlockSpec((1, rank), whole),
        ],
        out_specs=(
            pl.BlockSpec((1, rows, cols), by_block),
            pl.BlockSpec((rows, rank), whole),
            pl.BlockSpec((rows, rank), whole),
            pl.BlockSpec((1, rank), whole),
        ),
        compiler_params=pltpu.CompilerParams(vmem_limit_bytes=12 * 1024 * 1024),
    )(mall, cfull, appall, grads, applied, new_basis, eigen)
    return fresh[None], eigen, conditioned, applied_rows[None]


def solution(mesh):
    in_specs = (
        P("layer", "dp", None),
        P("layer", "dp", None),
        P("layer", "dp", None),
        P(None, "dp", "layer"),
    )
    out_specs = (
        P("layer", "dp", None),
        P("layer", None),
        P(None, "dp", "layer"),
        P("layer", "dp", None),
    )
    body = functools.partial(per_device, mesh.shape["layer"], mesh.shape["dp"])
    return jax.shard_map(body, mesh=mesh, in_specs=in_specs, out_specs=out_specs, check_vma=False)
```
